32 devices in a mesh: group: 4 (over y, x), local: 8 (over z, core).
Axes of the slice: x: 2, y: 2, z: 4, core: 2. Of those that a mesh axis runs over, the one named last changes fastest.
Arguments:
- tokens: bfloat16 [4096, 3584], P(('group', 'local')), may hold values from -6 to 6
- grad_out: bfloat16 [4096, 3584], P(('group', 'local')), may hold values from -6 to 6
- expert_ids: int32 [4096, 4], P(('group', 'local')), may hold values from 0 to 31, as said below
- combine: bfloat16 [4096, 4], P(('group', 'local')), may hold values from 0.099609375 to 1
- gate_weight: bfloat16 [32, 3584, 1024], P(('group', 'local')), may hold values from -0.09375 to 0.09375
- up_weight: bfloat16 [32, 3584, 1024], P(('group', 'local')), may hold values from -0.09375 to 0.09375
- down_weight: bfloat16 [32, 1024, 3584], P(('group', 'local')), may hold values from -0.1875 to 0.1875
Outputs:
- grad_tokens: bfloat16 [4096, 3584], P(('group', 'local'))
- grad_combine: bfloat16 [4096, 4], P(('group', 'local'))
The draws below stay inside these ranges and needn't reach their ends.
Inputs may be any that keep to these rules, and one draw needn't show every extreme that they name: `expert_ids`: each token names 4 different experts; expert e lies in node group e // 8. The first 2 experts of a token lie in one group and the other 2 in another, so a token uses 2 groups. The tokens of each device choose every group exactly 128//2 times. The tokens of one device name one expert at most 24 times, and in every draw some expert is named 24 times by the tokens of every device.
All inputs are finite; a program needn't handle non-finite values.
Results may differ from the reference program's by a relative error of at most 0.0058.
Values may be sent and summed in bfloat16 or wider, within the bound.
A program may use at most 128 MiB of HBM per device.

```python
import math
import jax
import jax.numpy as jnp
from jax import lax

D = 3584
FF = 1024
TOP = 4
TOK_DEV = 128
EXPERTS = 32
TOKENS = 4096
MEAN_PAIR = 16
PAIR_CAP = 24
N_GROUP = 4
N_LOCAL = 8


def draw_expert_ids(key, part):
    key_roles = jax.random.fold_in(key, 11)
    key_perm = jax.random.fold_in(key, 12)
    key_hot = jax.random.fold_in(key, 13)
    devices = N_GROUP * N_LOCAL
    roles = jax.vmap(lambda single: jax.random.permutation(single, TOK_DEV))(jax.random.split(key_roles, devices)).astype(jnp.int32)
    quarter = TOK_DEV // 4
    first = roles % 4
    within = roles // 4
    offset = jnp.where(within < 3 * quarter // 8, 1, jnp.where(within < 6 * quarter // 8, 3, 2))
    second = (first + offset) % 4
    rounds = MEAN_PAIR
    hot_rounds = (rounds + 1) // 2
    perms = jax.vmap(lambda single: jax.random.permutation(single, N_LOCAL))(jax.random.split(key_perm, devices * 4 * rounds))
    perms = perms.astype(jnp.int32).reshape(devices, 4, rounds, N_LOCAL)
    hottest = jax.random.randint(key_hot, (4,), 0, N_LOCAL).astype(jnp.int32)
    hot_block = hottest[None, :, None, None]
    position = jnp.argmax(perms == hot_block, axis=3).astype(jnp.int32)
    target = (position + 2) % N_LOCAL
    column = jnp.arange(N_LOCAL, dtype=jnp.int32)[None, None, None, :]
    round_index = jnp.arange(rounds, dtype=jnp.int32)[None, None, :, None]
    replace = (column == target[..., None]) & (round_index < hot_rounds)
    perms = jnp.where(replace, hot_block, perms)
    pool_flat = perms.reshape(devices, 4 * TOK_DEV)

    def choose(group, rank_in, shift):
        index = group * TOK_DEV + 2 * rank_in + shift
        return group * N_LOCAL + jnp.take_along_axis(pool_flat, index, axis=1)
    expert_zero = choose(first, within, 0)
    expert_one = choose(first, within, 1)
    expert_two = choose(second, quarter + within, 0)
    expert_three = choose(second, quarter + within, 1)
    stacked = jnp.stack([expert_zero, expert_one, expert_two, expert_three], axis=-1)
    return stacked.reshape(devices * TOK_DEV, 4).astype(jnp.int32)


def steps_of(stream_key, extent, shards, least, high):
    def one(axis_at, shards_of):
        heights = jax.random.uniform(jax.random.fold_in(jax.random.fold_in(stream_key, 6), axis_at), (shards_of,), jnp.float32, least / len(shards), high / len(shards))
        return jnp.repeat(jnp.exp(heights), extent[axis_at] // shards_of).reshape((-1,) + (1,) * (len(extent) - axis_at - 1))

    factor_of = one(*shards[0])
    for cut in shards[1:]:
        factor_of = factor_of * one(*cut)
    return factor_of


def noise(stream_key, dims, scale, most, shards=(), kind=jnp.bfloat16):
    array = scale * jax.random.normal(stream_key, dims, jnp.float32)
    if shards:
        array = array * steps_of(stream_key, dims, shards, -0.22, 0.18)
    return jnp.clip(array, -most, most).astype(kind)


def setup_inputs(seed: int = 0) -> dict:
    splits = jax.random.split(jax.random.key(seed), 8)
    tokens = noise(splits[0], (TOKENS, D), 1.0, 6.0, ((0, 32),))
    grad_out = noise(splits[1], (TOKENS, D), 1.0, 6.0, ((0, 32),))
    expert_ids = draw_expert_ids(jax.random.fold_in(splits[7], 71), 0)
    combine = jnp.clip(jnp.exp(math.log(1.0) - 2.306499 * jax.random.uniform(splits[3], (TOKENS, TOP), jnp.float32) ** steps_of(splits[3], (TOKENS, TOP), ((0, 32),), -0.2, 0.2)), 0.099609375, 1.0).astype(jnp.bfloat16)
    gate_weight = noise(splits[4], (EXPERTS, D, FF), D ** -0.5, 0.09375, ((0, 32),))
    up_weight = noise(splits[5], (EXPERTS, D, FF), D ** -0.5, 0.09375, ((0, 32),))
    down_weight = noise(splits[6], (EXPERTS, FF, D), FF ** -0.5, 0.1875, ((0, 32),))
    return {"tokens": tokens, "grad_out": grad_out, "expert_ids": expert_ids, "combine": combine, "gate_weight": gate_weight, "up_weight": up_weight, "down_weight": down_weight}


def expert_rows(rows_x, rows_dy, rows_p, gate_mat, up_mat, down_mat):
    gate_pre = jnp.dot(rows_x, gate_mat, preferred_element_type=jnp.float32)
    up_pre = jnp.dot(rows_x, up_mat, preferred_element_type=jnp.float32)
    sigmoid_gate = jax.nn.sigmoid(gate_pre)
    active = gate_pre * sigmoid_gate
    hidden = (active * up_pre).astype(jnp.bfloat16)
    output = jnp.dot(hidden, down_mat, preferred_element_type=jnp.float32)
    grad_weight = jnp.sum(rows_dy.astype(jnp.float32) * output, axis=1).astype(jnp.bfloat16)
    back_hidden = lax.dot_general(rows_dy, down_mat, (((1,), (1,)), ((), ())), preferred_element_type=jnp.float32)
    back_hidden = back_hidden * rows_p.astype(jnp.float32)[:, None]
    grad_gate = (back_hidden * up_pre * sigmoid_gate * (1.0 + gate_pre * (1.0 - sigmoid_gate))).astype(jnp.bfloat16)
    grad_up = (back_hidden * active).astype(jnp.bfloat16)
    contrib = lax.dot_general(grad_gate, gate_mat, (((1,), (1,)), ((), ())), preferred_element_type=jnp.float32)
    contrib = contrib + lax.dot_general(grad_up, up_mat, (((1,), (1,)), ((), ())), preferred_element_type=jnp.float32)
    return contrib.astype(jnp.bfloat16), grad_weight


def reference(tokens, grad_out, expert_ids, combine, gate_weight, up_weight, down_weight):
    flat_ids = expert_ids.reshape(-1).astype(jnp.int32)
    assign_count = flat_ids.shape[0]
    by_expert = jnp.argsort(flat_ids, stable=True).astype(jnp.int32)
    counts = jax.ops.segment_sum(jnp.ones((assign_count,), jnp.int32), flat_ids, num_segments=EXPERTS).astype(jnp.int32)
    starts = (jnp.cumsum(counts) - counts).astype(jnp.int32)
    capacity = EXPERTS * PAIR_CAP
    padded_order = jnp.concatenate([by_expert, jnp.zeros((capacity,), jnp.int32)])
    flat_weight = combine.reshape(-1)
    positions = jnp.arange(capacity, dtype=jnp.int32)

    def visit(state_pair, inputs):
        totals, weight_grads = state_pair
        expert, gate_mat, up_mat, down_mat = inputs
        picked = lax.dynamic_slice(padded_order, (starts[expert],), (capacity,))
        usable = positions < counts[expert]
        token_index = picked // TOP
        rows_x = jnp.where(usable[:, None], tokens[token_index], jnp.zeros((), tokens.dtype))
        rows_dy = jnp.where(usable[:, None], grad_out[token_index], jnp.zeros((), grad_out.dtype))
        rows_p = jnp.where(usable, flat_weight[picked], jnp.zeros((), combine.dtype))
        contrib, grad_weight = expert_rows(rows_x, rows_dy, rows_p, gate_mat, up_mat, down_mat)
        totals = totals.at[token_index].add(jnp.where(usable[:, None], contrib.astype(jnp.float32), 0.0))
        weight_grads = weight_grads.at[picked].add(jnp.where(usable, grad_weight.astype(jnp.float32), 0.0))
        return (totals, weight_grads), None

    initial = (jnp.zeros((TOKENS, D), jnp.float32), jnp.zeros((assign_count,), jnp.float32))
    final_state, _ = lax.scan(visit, initial, (jnp.arange(EXPERTS, dtype=jnp.int32), gate_weight, up_weight, down_weight))
    totals, weight_grads = final_state
    return totals.astype(jnp.bfloat16), weight_grads.reshape(TOKENS, TOP).astype(jnp.bfloat16)
```

```python
import jax
import jax.numpy as jnp
from jax import lax
from jax.sharding import PartitionSpec as P

F32 = jnp.float32
BF16 = jnp.bfloat16


def dot_t(left, right):
    return lax.dot_general(left, right, (((1,), (1,)), ((), ())), preferred_element_type=F32)


def forward_rows(rows_x, gate_mat, up_mat):
    gate_pre = jnp.dot(rows_x, gate_mat, preferred_element_type=F32)
    up_pre = jnp.dot(rows_x, up_mat, preferred_element_type=F32)
    return gate_pre, up_pre


def backward_rows(gate_pre, up_pre, rows_dy, gate_mat, up_mat, down_mat):
    back = dot_t(rows_dy, down_mat)
    sigmoid_gate = jax.nn.sigmoid(gate_pre)
    active = gate_pre * sigmoid_gate
    hidden = (active * up_pre).astype(BF16)
    grad_weight = jnp.sum(hidden.astype(F32) * back, axis=1).astype(BF16)
    grad_gate = (back * up_pre * sigmoid_gate * (1.0 + gate_pre * (1.0 - sigmoid_gate))).astype(BF16)
    grad_up = (back * active).astype(BF16)
    contrib = (dot_t(grad_gate, gate_mat) + dot_t(grad_up, up_mat)).astype(BF16)
    return contrib, grad_weight


def local(tokens, grad_out, expert_ids, combine, gate_weight, up_weight, down_weight):
    token_rows, model_width = tokens.shape
    top_count = expert_ids.shape[1]
    group_count = lax.axis_size("group")
    local_count = lax.axis_size("local")
    expert_count = group_count * local_count
    mean_pair = token_rows * top_count // expert_count
    pair_cap = mean_pair + (mean_pair + 1) // 2
    my_group = lax.axis_index("group")
    my_local = lax.axis_index("local")
    gate_mat, up_mat, down_mat = gate_weight[0], up_weight[0], down_weight[0]
    column_rows = local_count * token_rows
    pair_rows = local_count * pair_cap

    all_ids = lax.all_gather(expert_ids, "local", axis=0, tiled=True)
    all_combine = lax.all_gather(combine, "local", axis=0, tiled=True)
    all_x = lax.all_gather(tokens, "local", axis=0, tiled=True)
    all_dy = lax.all_gather(grad_out, "local", axis=0, tiled=True)

    partners = my_group ^ jnp.arange(group_count, dtype=jnp.int32)
    wanted = partners * local_count + my_local
    hit = all_ids[None, :, :] == wanted[:, None, None]
    named = jnp.any(hit, axis=2)
    weight = jnp.sum(jnp.where(hit, all_combine[None].astype(F32), 0.0), axis=2)
    counts = named.astype(jnp.int32).reshape(group_count, local_count, token_rows)
    rank = jnp.cumsum(counts, axis=2) - 1
    base = jnp.arange(local_count, dtype=jnp.int32)[None, :, None] * pair_cap
    slot = jnp.where(counts > 0, rank + base, -1).reshape(group_count, column_rows)
    slots = jnp.arange(pair_rows, dtype=jnp.int32)
    pick = slot[:, None, :] == slots[None, :, None]
    select = pick.astype(BF16)
    scatter = jnp.where(pick, weight[:, None, :], 0.0).astype(BF16)

    def swap(value, j):
        if j == 0:
            return value
        return lax.ppermute(value, "group", [(i, i ^ j) for i in range(group_count)])

    order = [j for j in range(group_count - 1, 0, -1)] + [0]

    def spread(column):
        moved = {}
        for j in order:
            rows = jnp.dot(select[j], column, preferred_element_type=F32).astype(BF16)
            moved[j] = swap(rows, j)
        return moved

    rows_x = spread(all_x)
    rows_dy = spread(all_dy)
    consume = [0] + [j for j in range(1, group_count)]
    pre = {j: forward_rows(rows_x[j], gate_mat, up_mat) for j in consume}
    back_rows, weights = {}, {}
    for j in consume:
        contrib, weights[j] = backward_rows(*pre[j], rows_dy[j], gate_mat, up_mat, down_mat)
        back_rows[j] = swap(contrib, j)

    total = lax.dot_general(
        scatter.reshape(group_count * pair_rows, column_rows),
        jnp.concatenate([back_rows[j] for j in range(group_count)], axis=0),
        (((0,), (0,)), ((), ())),
        preferred_element_type=F32,
    ).astype(BF16)
    grad_tokens = lax.psum_scatter(total, "local", scatter_dimension=0, tiled=True)

    grad_weight = jnp.stack([weights[j] for j in range(group_count)])[partners]
    grad_weight = grad_weight.reshape(expert_count, pair_cap)
    back_weight = lax.all_to_all(
        grad_weight, ("group", "local"), split_axis=0, concat_axis=0, tiled=True
    )
    flat_ids = expert_ids.reshape(-1)
    one_hot = flat_ids[:, None] == jnp.arange(expert_count, dtype=jnp.int32)[None, :]
    ranks = jnp.cumsum(one_hot.astype(jnp.int32), axis=0) - 1
    chosen = one_hot[:, :, None] & (
        ranks[:, :, None] == jnp.arange(pair_cap, dtype=jnp.int32)[None, None, :]
    )
    grad_combine = jnp.sum(jnp.where(chosen, back_weight[None].astype(F32), 0.0), axis=(1, 2))
    return grad_tokens, grad_combine.astype(BF16).reshape(token_rows, top_count)


def solution(mesh):
    rows = P(("group", "local"), None)
    mats = P(("group", "local"), None, None)
    return jax.shard_map(
        local,
        mesh=mesh,
        in_specs=(rows, rows, rows, rows, mats, mats, mats),
        out_specs=(rows, rows),
        check_vma=False,
    )
```

```python
import functools

import jax
import jax.numpy as jnp
from jax import lax
from jax.experimental import pallas as pl
from jax.experimental.pallas import tpu as pltpu
from jax.sharding import PartitionSpec as P

F32 = jnp.float32
BF16 = jnp.bfloat16


def dot_t(left, right):
    return lax.dot_general(left, right, (((1,), (1,)), ((), ())), preferred_element_type=F32)


def forward_rows(rows_x, gate_mat, up_mat):
    gate_pre = jnp.dot(rows_x, gate_mat, preferred_element_type=F32)
    up_pre = jnp.dot(rows_x, up_mat, preferred_element_type=F32)
    return gate_pre, up_pre


def backward_rows(gate_pre, up_pre, rows_dy, down_mat):
    back = dot_t(rows_dy, down_mat)
    sigmoid_gate = jax.nn.sigmoid(gate_pre)
    active = gate_pre * sigmoid_gate
    hidden = (active * up_pre).astype(BF16)
    grad_weight = jnp.sum(hidden.astype(F32) * back, axis=1).astype(BF16)
    grad_gate = (back * up_pre * sigmoid_gate * (1.0 + gate_pre * (1.0 - sigmoid_gate))).astype(BF16)
    grad_up = (back * active).astype(BF16)
    return grad_gate, grad_up, grad_weight


def partner_of(group, j):
    high = lax.rem(lax.div(group, 2) + j // 2, 2)
    low = lax.rem(lax.rem(group, 2) + j % 2, 2)
    return high * 2 + low


def exchange_kernel(tile, column_ref, select_ref, out_ref, picked, send_sem, recv_sem, own_sem):
    my_group, my_local = lax.axis_index("group"), lax.axis_index("local")
    width = picked.shape[2]
    barrier = pltpu.get_barrier_semaphore()
    for j in (1, 2, 3):
        pl.semaphore_signal(
            barrier,
            inc=1,
            device_id=(partner_of(my_group, j), my_local),
            device_id_type=pl.DeviceIdType.MESH,
        )
    pl.semaphore_wait(barrier, 3)

    def pick(j):
        @pl.loop(0, width // tile)
        def _(i):
            columns = pl.ds(pl.multiple_of(i * tile, tile), tile)
            picked[j, :, columns] = jnp.dot(
                select_ref[j], column_ref[:, columns], preferred_element_type=F32
            ).astype(BF16)

    copies = []
    for j in (3, 1, 2):
        pick(j)
        copy = pltpu.make_async_remote_copy(
            src_ref=picked.at[j],
            dst_ref=out_ref.at[j],
            send_sem=send_sem.at[j - 1],
            recv_sem=recv_sem.at[j - 1],
            device_id=(partner_of(my_group, j), my_local),
            device_id_type=pl.DeviceIdType.MESH,
        )
        copy.start()
        copies.append(copy)
    pick(0)
    own = pltpu.make_async_copy(picked.at[0], out_ref.at[0], own_sem)
    own.start()
    own.wait()
    for copy in copies:
        copy.wait()


def exchange(column, select, width, collective_id):
    groups, pair_rows, column_rows = select.shape
    return pl.pallas_call(
        functools.partial(exchange_kernel, 512),
        out_shape=jax.ShapeDtypeStruct((groups, pair_rows, width), BF16),
        in_specs=[pl.BlockSpec(memory_space=pltpu.VMEM)] * 2,
        out_specs=pl.BlockSpec(memory_space=pl.ANY),
        scratch_shapes=[
            pltpu.VMEM((groups, pair_rows, width), BF16),
            pltpu.SemaphoreType.DMA((3,)),
            pltpu.SemaphoreType.DMA((3,)),
            pltpu.SemaphoreType.DMA,
        ],
        compiler_params=pltpu.CompilerParams(
            collective_id=collective_id, has_side_effects=True, vmem_limit_bytes=40 * 2**20
        ),
        cost_estimate=pl.CostEstimate(
            flops=2 * groups * pair_rows * column_rows * width,
            bytes_accessed=2 * (column_rows * width + 2 * groups * pair_rows * width) * 8,
            transcendentals=0,
        ),
    )(column, select)


def local(tokens, grad_out, expert_ids, combine, gate_weight, up_weight, down_weight):
    token_rows, model_width = tokens.shape
    top_count = expert_ids.shape[1]
    group_count = lax.axis_size("group")
    local_count = lax.axis_size("local")
    expert_count = group_count * local_count
    mean_pair = token_rows * top_count // expert_count
    pair_cap = mean_pair + (mean_pair + 1) // 2
    my_group = lax.axis_index("group")
    my_local = lax.axis_index("local")
    gate_mat, up_mat, down_mat = gate_weight[0], up_weight[0], down_weight[0]
    column_rows = local_count * token_rows
    pair_rows = local_count * pair_cap

    extra = jnp.concatenate([expert_ids.astype(BF16), combine], axis=1)
    extra = jnp.pad(extra, ((0, 0), (0, 128 - 2 * top_count)))
    all_x = lax.all_gather(
        jnp.concatenate([tokens, extra], axis=1), "local", axis=0, tiled=True
    )
    all_dy = lax.all_gather(grad_out, "local", axis=0, tiled=True)
    all_ids = all_x[:, model_width : model_width + top_count].astype(jnp.int32)
    all_combine = all_x[:, model_width + top_count : model_width + 2 * top_count]

    partners = my_group ^ jnp.arange(group_count, dtype=jnp.int32)
    wanted = partners * local_count + my_local
    hit = all_ids[None, :, :] == wanted[:, None, None]
    named = jnp.any(hit, axis=2)
    weight = jnp.sum(jnp.where(hit, all_combine[None].astype(F32), 0.0), axis=2)
    counts = named.astype(jnp.int32).reshape(group_count, local_count, token_rows)
    rank = jnp.cumsum(counts, axis=2) - 1
    base = jnp.arange(local_count, dtype=jnp.int32)[None, :, None] * pair_cap
    slot = jnp.where(counts > 0, rank + base, -1).reshape(group_count, column_rows)
    slots = jnp.arange(pair_rows, dtype=jnp.int32)
    pick = slot[:, None, :] == slots[None, :, None]
    select = pick.astype(BF16)
    scatter = jnp.where(pick, weight[:, None, :], 0.0).astype(BF16)

    def swap(value, j):
        if j == 0:
            return value
        return lax.ppermute(value, "group", [(i, i ^ j) for i in range(group_count)])

    order = [j for j in range(group_count - 1, 0, -1)] + [0]

    fits = group_count == 4 and column_rows * model_width * 2 <= 12 * 2**20
    fits = fits and model_width % 512 == 0 and pair_rows % 16 == 0

    def spread(column, collective_id):
        if fits:
            return exchange(column, select, model_width, collective_id)
        moved = {}
        for j in order:
            picked = jnp.dot(select[j], column[:, :model_width], preferred_element_type=F32)
            moved[j] = swap(picked.astype(BF16), j)
        return moved

    rows_x = spread(all_x, 0)
    if fits:
        all_dy, rows_x = lax.optimization_barrier((all_dy, rows_x))
    rows_dy = spread(all_dy, 1)
    grads, weights = {}, {}
    for j in order:
        pre = forward_rows(rows_x[j], gate_mat, up_mat)
        *grads[j], weights[j] = backward_rows(*pre, rows_dy[j], down_mat)

    half = model_width // 2
    scatter = scatter.reshape(group_count * pair_rows, column_rows)
    parts = []
    for start in (0, half):
        back_rows = {}
        for j in order:
            gate_part = gate_mat[start : start + half]
            up_part = up_mat[start : start + half]
            contrib = (dot_t(grads[j][0], gate_part) + dot_t(grads[j][1], up_part)).astype(BF16)
            back_rows[j] = swap(contrib, j)
        total = lax.dot_general(
            scatter,
            jnp.concatenate([back_rows[j] for j in range(group_count)], axis=0),
            (((0,), (0,)), ((), ())),
            preferred_element_type=F32,
        ).astype(BF16)
        parts.append(lax.psum_scatter(total, "local", scatter_dimension=0, tiled=True))
    grad_tokens = jnp.concatenate(parts, axis=1)

    grad_weight = jnp.stack([weights[j] for j in range(group_count)])[partners]
    grad_weight = grad_weight.reshape(expert_count, pair_cap)
    back_weight = lax.all_to_all(
        grad_weight, ("group", "local"), split_axis=0, concat_axis=0, tiled=True
    )
    flat_ids = expert_ids.reshape(-1)
    one_hot = flat_ids[:, None] == jnp.arange(expert_count, dtype=jnp.int32)[None, :]
    ranks = jnp.cumsum(one_hot.astype(jnp.int32), axis=0) - 1
    chosen = one_hot[:, :, None] & (
        ranks[:, :, None] == jnp.arange(pair_cap, dtype=jnp.int32)[None, None, :]
    )
    grad_combine = jnp.sum(jnp.where(chosen, back_weight[None].astype(F32), 0.0), axis=(1, 2))
    return grad_tokens, grad_combine.astype(BF16).reshape(token_rows, top_count)


def solution(mesh):
    rows = P(("group", "local"), None)
    mats = P(("group", "local"), None, None)
    return jax.shard_map(
        local,
        mesh=mesh,
        in_specs=(rows, rows, rows, rows, mats, mats, mats),
        out_specs=(rows, rows),
        check_vma=False,
    )
```

```python
import functools

import jax
import jax.numpy as jnp
from jax import lax
from jax.experimental import pallas as pl
from jax.experimental.pallas import tpu as pltpu
from jax.sharding import PartitionSpec as P

F32 = jnp.float32
BF16 = jnp.bfloat16


def dot_t(left, right):
    return lax.dot_general(left, right, (((1,), (1,)), ((), ())), preferred_element_type=F32)


def forward_rows(rows_x, gate_mat, up_mat):
    gate_pre = jnp.dot(rows_x, gate_mat, preferred_element_type=F32)
    up_pre = jnp.dot(rows_x, up_mat, preferred_element_type=F32)
    return gate_pre, up_pre


def backward_rows(gate_pre, up_pre, rows_dy, down_mat):
    back = dot_t(rows_dy, down_mat)
    sigmoid_gate = jax.nn.sigmoid(gate_pre)
    active = gate_pre * sigmoid_gate
    hidden = (active * up_pre).astype(BF16)
    grad_weight = jnp.sum(hidden.astype(F32) * back, axis=1).astype(BF16)
    grad_gate = (back * up_pre * sigmoid_gate * (1.0 + gate_pre * (1.0 - sigmoid_gate))).astype(BF16)
    grad_up = (back * active).astype(BF16)
    return grad_gate, grad_up, grad_weight


def partner_of(group, j):
    high = lax.rem(lax.div(group, 2) + j // 2, 2)
    low = lax.rem(lax.rem(group, 2) + j % 2, 2)
    return high * 2 + low


def exchange_kernel(tile, column_ref, select_ref, out_ref, picked, send_sem, recv_sem, own_sem):
    my_group, my_local = lax.axis_index("group"), lax.axis_index("local")
    width = picked.shape[2]
    barrier = pltpu.get_barrier_semaphore()
    for j in (1, 2, 3):
        pl.semaphore_signal(
            barrier,
            inc=1,
            device_id=(partner_of(my_group, j), my_local),
            device_id_type=pl.DeviceIdType.MESH,
        )
    pl.semaphore_wait(barrier, 3)

    def pick(j):
        @pl.loop(0, width // tile)
        def _(i):
            columns = pl.ds(pl.multiple_of(i * tile, tile), tile)
            picked[j, :, columns] = jnp.dot(
                select_ref[j], column_ref[:, columns], preferred_element_type=F32
            ).astype(BF16)

    copies = []
    for j in (3, 1, 2):
        pick(j)
        copy = pltpu.make_async_remote_copy(
            src_ref=picked.at[j],
            dst_ref=out_ref.at[j],
            send_sem=send_sem.at[j - 1],
            recv_sem=recv_sem.at[j - 1],
            device_id=(partner_of(my_group, j), my_local),
            device_id_type=pl.DeviceIdType.MESH,
        )
        copy.start()
        copies.append(copy)
    pick(0)
    own = pltpu.make_async_copy(picked.at[0], out_ref.at[0], own_sem)
    own.start()
    own.wait()
    for copy in copies:
        copy.wait()


def exchange(column, select, width, collective_id):
    groups, pair_rows, column_rows = select.shape
    return pl.pallas_call(
        functools.partial(exchange_kernel, 512),
        out_shape=jax.ShapeDtypeStruct((groups, pair_rows, width), BF16),
        in_specs=[pl.BlockSpec(memory_space=pltpu.VMEM)] * 2,
        out_specs=pl.BlockSpec(memory_space=pl.ANY),
        scratch_shapes=[
            pltpu.VMEM((groups, pair_rows, width), BF16),
            pltpu.SemaphoreType.DMA((3,)),
            pltpu.SemaphoreType.DMA((3,)),
            pltpu.SemaphoreType.DMA,
        ],
        compiler_params=pltpu.CompilerParams(
            collective_id=collective_id, has_side_effects=True, vmem_limit_bytes=40 * 2**20
        ),
        cost_estimate=pl.CostEstimate(
            flops=2 * groups * pair_rows * column_rows * width,
            bytes_accessed=2 * (column_rows * width + 2 * groups * pair_rows * width) * 8,
            transcendentals=0,
        ),
    )(column, select)


def local(tokens, grad_out, expert_ids, combine, gate_weight, up_weight, down_weight):
    token_rows, model_width = tokens.shape
    top_count = expert_ids.shape[1]
    group_count = lax.axis_size("group")
    local_count = lax.axis_size("local")
    expert_count = group_count * local_count
    mean_pair = token_rows * top_count // expert_count
    pair_cap = mean_pair + (mean_pair + 1) // 2
    my_group = lax.axis_index("group")
    my_local = lax.axis_index("local")
    gate_mat, up_mat, down_mat = gate_weight[0], up_weight[0], down_weight[0]
    column_rows = local_count * token_rows
    pair_rows = local_count * pair_cap

    extra = jnp.concatenate([expert_ids.astype(BF16), combine], axis=1)
    extra = jnp.pad(extra, ((0, 0), (0, 128 - 2 * top_count)))
    all_x = lax.all_gather(
        jnp.concatenate([tokens, extra], axis=1), "local", axis=0, tiled=True
    )
    all_dy = lax.all_gather(grad_out, "local", axis=0, tiled=True)
    all_ids = all_x[:, model_width : model_width + top_count].astype(jnp.int32)
    all_combine = all_x[:, model_width + top_count : model_width + 2 * top_count]

    partners = my_group ^ jnp.arange(group_count, dtype=jnp.int32)
    wanted = partners * local_count + my_local
    hit = all_ids[None, :, :] == wanted[:, None, None]
    named = jnp.any(hit, axis=2)
    weight = jnp.sum(jnp.where(hit, all_combine[None].astype(F32), 0.0), axis=2)
    counts = named.astype(jnp.int32).reshape(group_count, local_count, token_rows)
    rank = jnp.cumsum(counts, axis=2) - 1
    base = jnp.arange(local_count, dtype=jnp.int32)[None, :, None] * pair_cap
    slot = jnp.where(counts > 0, rank + base, -1).reshape(group_count, column_rows)
    slots = jnp.arange(pair_rows, dtype=jnp.int32)
    pick = slot[:, None, :] == slots[None, :, None]
    select = pick.astype(BF16)
    scatter = jnp.where(pick, weight[:, None, :], 0.0).astype(BF16)

    def swap(value, j):
        if j == 0:
            return value
        return lax.ppermute(value, "group", [(i, i ^ j) for i in range(group_count)])

    order = [j for j in range(group_count - 1, 0, -1)] + [0]

    fits = group_count == 4 and column_rows * model_width * 2 <= 12 * 2**20
    fits = fits and model_width % 512 == 0 and pair_rows % 16 == 0

    def spread(column, by_kernel):
        if by_kernel:
            return exchange(column, select, model_width, 0)
        moved = {}
        for j in order:
            picked = jnp.dot(select[j], column[:, :model_width], preferred_element_type=F32)
            moved[j] = swap(picked.astype(BF16), j)
        return moved

    rows_x = spread(all_x, fits)
    if fits:
        all_dy, rows_x = lax.optimization_barrier((all_dy, rows_x))
    rows_dy = spread(all_dy, False)
    grads, weights = {}, {}
    for j in order:
        pre = forward_rows(rows_x[j], gate_mat, up_mat)
        *grads[j], weights[j] = backward_rows(*pre, rows_dy[j], down_mat)

    half = model_width // 2
    scatter = scatter.reshape(group_count * pair_rows, column_rows)
    parts = []
    for start in (0, half):
        back_rows = {}
        for j in order:
            gate_part = gate_mat[start : start + half]
            up_part = up_mat[start : start + half]
            contrib = (dot_t(grads[j][0], gate_part) + dot_t(grads[j][1], up_part)).astype(BF16)
            back_rows[j] = swap(contrib, j)
        total = lax.dot_general(
            scatter,
            jnp.concatenate([back_rows[j] for j in range(group_count)], axis=0),
            (((0,), (0,)), ((), ())),
            preferred_element_type=F32,
        ).astype(BF16)
        parts.append(lax.psum_scatter(total, "local", scatter_dimension=0, tiled=True))
    grad_tokens = jnp.concatenate(parts, axis=1)

    grad_weight = jnp.stack([weights[j] for j in range(group_count)])[partners]
    grad_weight = grad_weight.reshape(expert_count, pair_cap)
    back_weight = lax.all_to_all(
        grad_weight, ("group", "local"), split_axis=0, concat_axis=0, tiled=True
    )
    flat_ids = expert_ids.reshape(-1)
    one_hot = flat_ids[:, None] == jnp.arange(expert_count, dtype=jnp.int32)[None, :]
    ranks = jnp.cumsum(one_hot.astype(jnp.int32), axis=0) - 1
    chosen = one_hot[:, :, None] & (
        ranks[:, :, None] == jnp.arange(pair_cap, dtype=jnp.int32)[None, None, :]
    )
    grad_combine = jnp.sum(jnp.where(chosen, back_weight[None].astype(F32), 0.0), axis=(1, 2))
    return grad_tokens, grad_combine.astype(BF16).reshape(token_rows, top_count)


def solution(mesh):
    rows = P(("group", "local"), None)
    mats = P(("group", "local"), None, None)
    return jax.shard_map(
        local,
        mesh=mesh,
        in_specs=(rows, rows, rows, rows, mats, mats, mats),
        out_specs=(rows, rows),
        check_vma=False,
    )
```
